32 devices in a mesh: gx: 2 (over x), gy: 4 (over z), gz: 4 (over y, core).
Axes of the slice: x: 2, y: 2, z: 4, core: 2. Of those that a mesh axis runs over, the one named last changes fastest.
Arguments:
- initial_block: float32 [64, 32, 32, 256], P(None, 'gz', 'gy', 'gx'), may hold values from -6 to 6
- phase_map: int32 [32, 32, 256], P('gz', 'gy', 'gx'), may hold values from 0 to 3
- phase_density: float32 [4], replicated, may hold values from 0.5 to 4
- phase_modulus: float32 [4], replicated, may hold values from 0.5 to 4
- bloch_sign: int32 [32, 256], P('gy', 'gx'), may hold values from -1 to 1, as said below
Outputs:
- ritz_basis: float32 [64, 32, 32, 256], P(None, 'gz', 'gy', 'gx')
- projected: float32 [64, 64], replicated
The draws below stay inside these ranges and needn't reach their ends.
Inputs may be any that keep to these rules, and one draw needn't show every extreme that they name: `bloch_sign`: each entry is -1 or +1.
All inputs are finite; a program needn't handle non-finite values.
Results may differ from the reference program's by a relative error of at most 0.00011.
Values sent between devices are 32-bit elements; how exact they have to be, the bound alone decides.
A program may use at most 128 MiB of HBM per device.

```python
import math
import jax
import jax.numpy as jnp
from jax import lax

K = 64
DEGREE = 6
PHASES = 4
NX = 256
NY = 32
NZ = 32
CELLS = 262144


def draw_bloch_sign(key, part):
    return (2 * jax.random.randint(key, (NY, NX), 0, 2) - 1).astype(jnp.int32)


def plant(drawn, own_key, low, high):
    longest = drawn.shape.index(max(drawn.shape))
    spots = []
    for shift in (0, 1):
        where = [jax.random.randint(jax.random.fold_in(own_key, axis), (), 0, length) for axis, length in enumerate(drawn.shape)]
        where[longest] = (where[longest] + shift) % drawn.shape[longest]
        spots.append(tuple(where))
    return drawn.at[spots[0]].set(low).at[spots[1]].set(high)


def shard_levels(own_key, shape, shards, smallest, high):
    def one(dim, parts):
        draws = jax.random.uniform(jax.random.fold_in(jax.random.fold_in(own_key, 6), dim), (parts,), jnp.float32, smallest / len(shards), high / len(shards))
        return jnp.repeat(jnp.exp(draws), shape[dim] // parts).reshape((-1,) + (1,) * (len(shape) - dim - 1))

    level = one(*shards[0])
    for cut in shards[1:]:
        level = level * one(*cut)
    return level


def centred(stream_key, shape, width, reach, shards=(), kind=jnp.bfloat16):
    values = jax.random.normal(stream_key, shape, jnp.float32) * width
    if len(shards) > 0:
        values = shard_levels(stream_key, shape, shards, -0.22, 0.18) * values
    return jnp.clip(values, min=-reach, max=reach).astype(kind)


def setup_inputs(seed: int = 0) -> dict:
    key_of = jax.random.split(jax.random.key(seed), 6)
    return {
        "initial_block": centred(key_of[0], (K, NZ, NY, NX), 1.0, 6.0, ((1, 4), (2, 4), (3, 2)), jnp.float32),
        "phase_map": plant(jax.random.randint(key_of[1], (NZ, NY, NX), 0, PHASES), jax.random.fold_in(key_of[1], 1), 0, PHASES - 1).astype(jnp.int32),
        "phase_density": jnp.clip(jnp.exp(jax.random.uniform(key_of[2], (PHASES,), jnp.float32, math.log(0.5), math.log(4.0))), 0.5, 4.0),
        "phase_modulus": jnp.clip(jnp.exp(jax.random.uniform(key_of[3], (PHASES,), jnp.float32, math.log(0.5), math.log(4.0))), 0.5, 4.0),
        "bloch_sign": draw_bloch_sign(jax.random.fold_in(key_of[5], 71), 0),
    }


def lookup(phase_map, table):
    hits = phase_map[..., None] == jnp.arange(PHASES, dtype=jnp.int32)
    return jnp.sum(jnp.where(hits, table, jnp.float32(0.0)), axis=-1)

def stiffness(field, inv_rho, sign):
    total = None
    for axis in (0, 1, 2):
        after = jnp.roll(field, -1, axis)
        before = jnp.roll(field, 1, axis)
        if axis == 0:
            after = after.at[-1].multiply(sign)
            before = before.at[0].multiply(sign)
        w_up = 0.5 * (inv_rho + jnp.roll(inv_rho, -1, axis))
        w_down = 0.5 * (inv_rho + jnp.roll(inv_rho, 1, axis))
        term = w_up * (field - after) + w_down * (field - before)
        total = term if total is None else total + term
    return total

def reference(initial_block, phase_map, phase_density, phase_modulus, bloch_sign):
    inv_rho = lookup(phase_map, 1.0 / phase_density)
    kappa = lookup(phase_map, phase_modulus)
    sign = bloch_sign.astype(jnp.float32)
    top = 12.0 * jnp.max(phase_modulus) * jnp.max(1.0 / phase_density)
    low = 0.03 * top
    centre = (top + low) / 2.0
    half = (top - low) / 2.0

    def filtered_one(vector):
        current = vector
        lap = kappa * stiffness(current, inv_rho, sign)
        following = (lap - centre * current) / half
        previous, current = (current, following)
        for step in range(DEGREE - 1):
            lap = kappa * stiffness(current, inv_rho, sign)
            following = 2.0 * (lap - centre * current) / half - previous
            previous, current = (current, following)
        return (current, stiffness(current, inv_rho, sign))
    filtered, applied = lax.map(filtered_one, initial_block)
    flat = filtered.reshape(K, -1)
    weighted = flat / kappa.reshape(1, -1)
    correlation = jnp.dot(weighted, flat.T, precision=lax.Precision.HIGHEST) / CELLS
    energy = jnp.dot(flat, applied.reshape(K, -1).T, precision=lax.Precision.HIGHEST) / CELLS
    factor = jnp.linalg.cholesky(correlation)
    inverse = jax.scipy.linalg.solve_triangular(factor, jnp.eye(K, dtype=jnp.float32), lower=True)
    basis = jnp.dot(inverse, flat, precision=lax.Precision.HIGHEST).reshape(filtered.shape)
    projected = jnp.dot(jnp.dot(inverse, energy, precision=lax.Precision.HIGHEST), inverse.T, precision=lax.Precision.HIGHEST)
    return (basis, projected)
```

```python
import functools

import jax
import jax.numpy as jnp
from jax import lax
from jax.experimental import pallas as pl
from jax.experimental.pallas import tpu as pltpu
from jax.sharding import PartitionSpec as P

DEGREE = 6
GROUPS = 2
SUB, LANE = 8, 128
MESH = pl.DeviceIdType.MESH


def lookup(phase_map, table):
    hits = phase_map[..., None] == jnp.arange(table.shape[0], dtype=jnp.int32)
    return jnp.sum(jnp.where(hits, table, jnp.float32(0.0)), axis=-1)


def filter_kernel(
    scal_ref, init_ref, rho_ref, kappa_ref, low_ref, high_ref,
    filt_ref, app_ref,
    wcoef, vcoef, sendz, sendy, sendx, haloz, haloy, halox, send_sem, recv_sem,
):
    rows, nz = init_ref.shape[0], init_ref.shape[1]
    size = rows // GROUPS
    spans = [(g * size, size) for g in range(GROUPS)] + [(rows, 1)]
    gx, gy, gz = (lax.axis_index(a) for a in ("gx", "gy", "gz"))
    cx, cy, cz = (lax.axis_size(a) for a in ("gx", "gy", "gz"))
    other_x = (lax.rem(gx + 1, cx), gy, gz)
    y_up = (gx, lax.rem(gy + 1, cy), gz)
    y_down = (gx, lax.rem(gy + cy - 1, cy), gz)
    z_up = (gx, gy, lax.rem(gz + 1, cz))
    z_down = (gx, gy, lax.rem(gz + cz - 1, cz))

    barrier = pltpu.get_barrier_semaphore()
    for device in (other_x, y_up, y_down, z_up, z_down):
        pl.semaphore_signal(barrier, inc=1, device_id=device, device_id_type=MESH)
    pl.semaphore_wait(barrier, 5)

    lane = lax.broadcasted_iota(jnp.int32, (SUB, LANE), 1)
    sub = lax.broadcasted_iota(jnp.int32, (SUB, LANE), 0)

    def copies(slot, g):
        start, length = spans[g]
        part = pl.ds(start, length)
        plan = (
            (sendy.at[0, part], haloy.at[slot, 1, part], y_down),
            (sendy.at[1, part], haloy.at[slot, 0, part], y_up),
            (sendz.at[0, part], haloz.at[slot, 1, part], z_down),
            (sendz.at[1, part], haloz.at[slot, 0, part], z_up),
            (sendx.at[part], halox.at[slot, part], other_x),
        )
        return [
            pltpu.make_async_remote_copy(
                src_ref=src, dst_ref=dst,
                send_sem=send_sem.at[g, i], recv_sem=recv_sem.at[slot, g, i],
                device_id=device, device_id_type=MESH,
            )
            for i, (src, dst, device) in enumerate(plan)
        ]

    def pack(tiles, k):
        sendz[0, k] = tiles[0]
        sendz[1, k] = tiles[-1]
        packed = jnp.zeros((SUB, LANE), jnp.float32)
        for z, tile in enumerate(tiles):
            sendy[0, k, z : z + 1, :] = tile[0:1]
            sendy[1, k, z : z + 1, :] = tile[SUB - 1 : SUB]
            first = pltpu.roll(tile, 2 * z, 1) if z else tile
            packed = jnp.where(lane == 2 * z, first, packed)
            packed = jnp.where(lane == 2 * z + 1, pltpu.roll(tile, 2 * z + 2, 1), packed)
        sendx[k] = packed

    def neighbours(tiles, k, slot, z):
        tile = tiles[z]
        up = tiles[z + 1] if z + 1 < nz else haloz[slot, 1, k]
        down = tiles[z - 1] if z else haloz[slot, 0, k]
        y_after = jnp.where(
            sub == SUB - 1, haloy[slot, 1, k, z : z + 1, :], pltpu.roll(tile, SUB - 1, 0)
        )
        y_before = jnp.where(sub == 0, haloy[slot, 0, k, z : z + 1, :], pltpu.roll(tile, 1, 0))
        edge = pltpu.roll(halox[slot, k], LANE - 2 * z - 1, 1)
        x_after = jnp.where(lane == LANE - 1, edge, pltpu.roll(tile, LANE - 1, 1))
        x_before = jnp.where(lane == 0, edge, pltpu.roll(tile, 1, 1))
        return up, down, y_after, y_before, x_after, x_before

    def send(slot, g):
        for copy in copies(slot, g):
            copy.start()

    def arrive(slot, g):
        for copy in copies(slot, g):
            copy.wait()

    pack([rho_ref[z] for z in range(nz)], rows)
    send(0, GROUPS)
    for g in range(GROUPS):
        start, length = spans[g]

        def first(i, carry):
            k = start + i
            pack([init_ref[k, z] for z in range(nz)], k)
            return carry

        lax.fori_loop(0, length, first, 0)
        send(0, g)

    arrive(0, GROUPS)
    scale, shift = scal_ref[0], scal_ref[1]
    tiles = [rho_ref[z] for z in range(nz)]
    for z in range(nz):
        weights = [0.5 * (tiles[z] + n) for n in neighbours(tiles, rows, 0, z)]
        total = weights[0] + weights[1]
        for w in weights[2:]:
            total = total + w
        if z == nz - 1:
            weights[0] = weights[0] * high_ref[...]
        if z == 0:
            weights[1] = weights[1] * low_ref[...]
        factor = scale * kappa_ref[z]
        for i, w in enumerate(weights):
            wcoef[i, z] = w
            vcoef[i, z] = factor * w
        wcoef[6, z] = total
        vcoef[6, z] = factor * total - shift

    for step in range(DEGREE + 1):
        slot = step % 2
        last = step == DEGREE
        current = init_ref if step == 0 else (app_ref if step % 2 else filt_ref)
        target = app_ref if step % 2 == 0 else filt_ref
        previous = None
        if 0 < step < DEGREE:
            previous = init_ref if step == 1 else target
        coef = wcoef if last else vcoef
        for g in range(GROUPS):
            start, length = spans[g]
            arrive(slot, g)

            def one(i, carry):
                k = start + i
                tiles = [current[k, z] for z in range(nz)]
                made = []
                for z in range(nz):
                    around = neighbours(tiles, k, slot, z)
                    terms = [coef[j, z] * n for j, n in enumerate(around)]
                    pairs = (terms[0] + terms[1]) + (terms[2] + terms[3])
                    value = coef[6, z] * tiles[z] - (pairs + (terms[4] + terms[5]))
                    if step == 0:
                        value = 0.5 * value
                    if previous is not None:
                        value = value - previous[k, z]
                    made.append(value)
                for z in range(nz):
                    target[k, z] = made[z]
                if not last:
                    pack(made, k)
                return carry

            lax.fori_loop(0, length, one, 0)
            if not last:
                send(1 - slot, g)


def filtered_block(scal, block, inv_rho, kappa, low, high):
    rows = block.shape[0]
    vmem = pl.BlockSpec(memory_space=pltpu.VMEM)
    nz = block.shape[1]
    f32 = jnp.float32
    return pl.pallas_call(
        filter_kernel,
        out_shape=[jax.ShapeDtypeStruct(block.shape, f32)] * 2,
        in_specs=[pl.BlockSpec(memory_space=pltpu.SMEM)] + [vmem] * 5,
        out_specs=[vmem] * 2,
        scratch_shapes=[
            pltpu.VMEM((7, nz, SUB, LANE), f32),
            pltpu.VMEM((7, nz, SUB, LANE), f32),
            pltpu.VMEM((2, rows + 1, SUB, LANE), f32),
            pltpu.VMEM((2, rows + 1, SUB, LANE), f32),
            pltpu.VMEM((rows + 1, SUB, LANE), f32),
            pltpu.VMEM((2, 2, rows + 1, SUB, LANE), f32),
            pltpu.VMEM((2, 2, rows + 1, SUB, LANE), f32),
            pltpu.VMEM((2, rows + 1, SUB, LANE), f32),
            pltpu.SemaphoreType.DMA((GROUPS + 1, 5)),
            pltpu.SemaphoreType.DMA((2, GROUPS + 1, 5)),
        ],
        compiler_params=pltpu.CompilerParams(
            collective_id=0, has_side_effects=True, vmem_limit_bytes=40 * 1024 * 1024
        ),
    )(scal, block, inv_rho, kappa, low, high)


def gram(left, right):
    rows = left.shape[0]
    return jnp.dot(
        left.reshape(rows, -1), right.reshape(rows, -1).T, precision=lax.Precision.HIGHEST
    )


def body(initial_block, phase_map, phase_density, phase_modulus, bloch_sign):
    inv_rho = lookup(phase_map, 1.0 / phase_density)
    kappa = lookup(phase_map, phase_modulus)
    sign = bloch_sign.astype(jnp.float32)
    z_index = lax.axis_index("gz")
    z_count = lax.axis_size("gz")
    low_factor = jnp.where(z_index == 0, sign, jnp.float32(1.0))
    high_factor = jnp.where(z_index == z_count - 1, sign, jnp.float32(1.0))
    top = 12.0 * jnp.max(phase_modulus) * jnp.max(1.0 / phase_density)
    low = 0.03 * top
    centre = (top + low) / 2.0
    half = (top - low) / 2.0
    cells = (
        initial_block.shape[1]
        * initial_block.shape[2]
        * initial_block.shape[3]
        * lax.axis_size("gx")
        * lax.axis_size("gy")
        * z_count
    )
    scal = jnp.stack([2.0 / half, 2.0 * centre / half])
    current, applied = filtered_block(scal, initial_block, inv_rho, kappa, low_factor, high_factor)
    correlation_local = gram(current / kappa[None], current)
    energy_local = gram(current, applied)
    correlation_total, energy_total = lax.psum(
        (correlation_local, energy_local), ("gx", "gy", "gz")
    )
    correlation = correlation_total / cells
    energy = energy_total / cells
    rows = current.shape[0]
    factor = jnp.linalg.cholesky(correlation)
    inverse = jax.scipy.linalg.solve_triangular(
        factor, jnp.eye(rows, dtype=jnp.float32), lower=True
    )
    basis = jnp.dot(inverse, current.reshape(rows, -1), precision=lax.Precision.HIGHEST).reshape(
        current.shape
    )
    projected = jnp.dot(
        jnp.dot(inverse, energy, precision=lax.Precision.HIGHEST),
        inverse.T,
        precision=lax.Precision.HIGHEST,
    )
    return (basis, projected)


def solution(mesh):
    in_specs = (P(None, "gz", "gy", "gx"), P("gz", "gy", "gx"), P(), P(), P("gy", "gx"))
    out_specs = (P(None, "gz", "gy", "gx"), P())
    return jax.shard_map(body, mesh=mesh, in_specs=in_specs, out_specs=out_specs, check_vma=False)
```

```python
import functools

import jax
import jax.numpy as jnp
from jax import lax
from jax.experimental import pallas as pl
from jax.experimental.pallas import tpu as pltpu
from jax.sharding import PartitionSpec as P

DEGREE = 6
GROUPS = 4
SUB, LANE = 8, 128
MESH = pl.DeviceIdType.MESH


def lookup(phase_map, table):
    hits = phase_map[..., None] == jnp.arange(table.shape[0], dtype=jnp.int32)
    return jnp.sum(jnp.where(hits, table, jnp.float32(0.0)), axis=-1)


def filter_kernel(
    scal_ref, init_ref, rho_ref, kappa_ref, low_ref, high_ref,
    filt_ref, both_ref,
    app_ref, wcoef, vcoef, sendz, sendy, sendx, haloz, haloy, halox, send_sem, recv_sem,
):
    rows, nz = init_ref.shape[0], init_ref.shape[1]
    size = rows // GROUPS
    spans = [(g * size, size) for g in range(GROUPS)] + [(rows, 1)]
    gx, gy, gz = (lax.axis_index(a) for a in ("gx", "gy", "gz"))
    cx, cy, cz = (lax.axis_size(a) for a in ("gx", "gy", "gz"))
    other_x = (lax.rem(gx + 1, cx), gy, gz)
    y_up = (gx, lax.rem(gy + 1, cy), gz)
    y_down = (gx, lax.rem(gy + cy - 1, cy), gz)
    z_up = (gx, gy, lax.rem(gz + 1, cz))
    z_down = (gx, gy, lax.rem(gz + cz - 1, cz))

    barrier = pltpu.get_barrier_semaphore()
    for device in (other_x, y_up, y_down, z_up, z_down):
        pl.semaphore_signal(barrier, inc=1, device_id=device, device_id_type=MESH)
    pl.semaphore_wait(barrier, 5)

    lane = lax.broadcasted_iota(jnp.int32, (SUB, LANE), 1)
    sub = lax.broadcasted_iota(jnp.int32, (SUB, LANE), 0)

    def copies(slot, g):
        start, length = spans[g]
        part = pl.ds(start, length)
        plan = (
            (sendy.at[0, part], haloy.at[slot, 1, part], y_down),
            (sendy.at[1, part], haloy.at[slot, 0, part], y_up),
            (sendz.at[0, part], haloz.at[slot, 1, part], z_down),
            (sendz.at[1, part], haloz.at[slot, 0, part], z_up),
            (sendx.at[part], halox.at[slot, part], other_x),
        )
        return [
            pltpu.make_async_remote_copy(
                src_ref=src, dst_ref=dst,
                send_sem=send_sem.at[g, i], recv_sem=recv_sem.at[slot, g, i],
                device_id=device, device_id_type=MESH,
            )
            for i, (src, dst, device) in enumerate(plan)
        ]

    def pack(tiles, k):
        sendz[0, k] = tiles[0]
        sendz[1, k] = tiles[-1]
        packed = jnp.zeros((SUB, LANE), jnp.float32)
        for z, tile in enumerate(tiles):
            sendy[0, k, z : z + 1, :] = tile[0:1]
            sendy[1, k, z : z + 1, :] = tile[SUB - 1 : SUB]
            first = pltpu.roll(tile, 2 * z, 1) if z else tile
            packed = jnp.where(lane == 2 * z, first, packed)
            packed = jnp.where(lane == 2 * z + 1, pltpu.roll(tile, 2 * z + 2, 1), packed)
        sendx[k] = packed

    def neighbours(tiles, k, slot, z):
        tile = tiles[z]
        up = tiles[z + 1] if z + 1 < nz else haloz[slot, 1, k]
        down = tiles[z - 1] if z else haloz[slot, 0, k]
        y_after = jnp.where(
            sub == SUB - 1, haloy[slot, 1, k, z : z + 1, :], pltpu.roll(tile, SUB - 1, 0)
        )
        y_before = jnp.where(sub == 0, haloy[slot, 0, k, z : z + 1, :], pltpu.roll(tile, 1, 0))
        edge = pltpu.roll(halox[slot, k], LANE - 2 * z - 1, 1)
        x_after = jnp.where(lane == LANE - 1, edge, pltpu.roll(tile, LANE - 1, 1))
        x_before = jnp.where(lane == 0, edge, pltpu.roll(tile, 1, 1))
        return up, down, y_after, y_before, x_after, x_before

    def send(slot, g):
        for copy in copies(slot, g):
            copy.start()

    def arrive(slot, g):
        for copy in copies(slot, g):
            copy.wait()

    pack([rho_ref[z] for z in range(nz)], rows)
    send(0, GROUPS)
    for g in range(GROUPS):
        start, length = spans[g]

        def first(i, carry):
            k = start + i
            pack([init_ref[k, z] for z in range(nz)], k)
            return carry

        lax.fori_loop(0, length, first, 0)
        send(0, g)

    arrive(0, GROUPS)
    scale, shift = scal_ref[0], scal_ref[1]
    tiles = [rho_ref[z] for z in range(nz)]
    for z in range(nz):
        weights = [0.5 * (tiles[z] + n) for n in neighbours(tiles, rows, 0, z)]
        total = weights[0] + weights[1]
        for w in weights[2:]:
            total = total + w
        if z == nz - 1:
            weights[0] = weights[0] * high_ref[...]
        if z == 0:
            weights[1] = weights[1] * low_ref[...]
        factor = scale * kappa_ref[z]
        for i, w in enumerate(weights):
            wcoef[i, z] = w
            vcoef[i, z] = factor * w
        wcoef[6, z] = total
        wcoef[7, z] = 1.0 / kappa_ref[z]
        vcoef[6, z] = factor * total - shift

    for step in range(DEGREE + 1):
        slot = step % 2
        last = step == DEGREE
        current = init_ref if step == 0 else (app_ref if step % 2 else filt_ref)
        target = app_ref if step % 2 == 0 else filt_ref
        previous = None
        if 0 < step < DEGREE:
            previous = init_ref if step == 1 else target
        coef = wcoef if last else vcoef
        for g in range(GROUPS):
            start, length = spans[g]
            arrive(slot, g)

            def one(i, carry):
                k = start + i
                tiles = [current[k, z] for z in range(nz)]
                made = []
                for z in range(nz):
                    around = neighbours(tiles, k, slot, z)
                    terms = [coef[j, z] * n for j, n in enumerate(around)]
                    pairs = (terms[0] + terms[1]) + (terms[2] + terms[3])
                    value = coef[6, z] * tiles[z] - (pairs + (terms[4] + terms[5]))
                    if step == 0:
                        value = 0.5 * value
                    if previous is not None:
                        value = value - previous[k, z]
                    made.append(value)
                if last:
                    for z in range(nz):
                        both_ref[k, z] = tiles[z] * wcoef[7, z]
                        both_ref[rows + k, z] = made[z]
                else:
                    for z in range(nz):
                        target[k, z] = made[z]
                    pack(made, k)
                return carry

            lax.fori_loop(0, length, one, 0)
            if not last:
                send(1 - slot, g)


def filtered_block(scal, block, inv_rho, kappa, low, high):
    rows = block.shape[0]
    vmem = pl.BlockSpec(memory_space=pltpu.VMEM)
    nz = block.shape[1]
    f32 = jnp.float32
    return pl.pallas_call(
        filter_kernel,
        out_shape=[
            jax.ShapeDtypeStruct(block.shape, f32),
            jax.ShapeDtypeStruct((2 * rows,) + block.shape[1:], f32),
        ],
        in_specs=[pl.BlockSpec(memory_space=pltpu.SMEM)] + [vmem] * 5,
        out_specs=[vmem] * 2,
        scratch_shapes=[
            pltpu.VMEM(block.shape, f32),
            pltpu.VMEM((8, nz, SUB, LANE), f32),
            pltpu.VMEM((7, nz, SUB, LANE), f32),
            pltpu.VMEM((2, rows + 1, SUB, LANE), f32),
            pltpu.VMEM((2, rows + 1, SUB, LANE), f32),
            pltpu.VMEM((rows + 1, SUB, LANE), f32),
            pltpu.VMEM((2, 2, rows + 1, SUB, LANE), f32),
            pltpu.VMEM((2, 2, rows + 1, SUB, LANE), f32),
            pltpu.VMEM((2, rows + 1, SUB, LANE), f32),
            pltpu.SemaphoreType.DMA((GROUPS + 1, 5)),
            pltpu.SemaphoreType.DMA((2, GROUPS + 1, 5)),
        ],
        compiler_params=pltpu.CompilerParams(
            collective_id=0, has_side_effects=True, vmem_limit_bytes=40 * 1024 * 1024
        ),
    )(scal, block, inv_rho, kappa, low, high)


def sum_kernel(local_ref, out_ref, *scratch):
    axes = ("gx", "gy", "gz")
    buffers, sends, arrivals = scratch[:3], scratch[3:6], scratch[6:9]
    places = {a: lax.axis_index(a) for a in axes}
    counts = {a: lax.axis_size(a) for a in axes}

    def partner(axis, distance):
        count = counts[axis]
        place = dict(places)
        place[axis] = lax.rem(places[axis] + distance, count)
        return tuple(place[a] for a in axes)

    barrier = pltpu.get_barrier_semaphore()
    greeted = 0
    for axis in axes:
        for distance in range(1, counts[axis]):
            pl.semaphore_signal(
                barrier, inc=1, device_id=partner(axis, distance), device_id_type=MESH
            )
            greeted += 1
    pl.semaphore_wait(barrier, greeted)

    value = local_ref[...]
    for axis, buffer, send_sem, recv_sem in zip(axes, buffers, sends, arrivals):
        me = places[axis]
        buffer[me] = value
        started = []
        for distance in range(1, counts[axis]):
            copy = pltpu.make_async_remote_copy(
                src_ref=buffer.at[me], dst_ref=buffer.at[me],
                send_sem=send_sem.at[distance], recv_sem=recv_sem.at[distance],
                device_id=partner(axis, distance), device_id_type=MESH,
            )
            copy.start()
            started.append(copy)
        for distance, copy in enumerate(started, 1):
            copy.wait_send()
            source = lax.rem(me + counts[axis] - distance, counts[axis])
            pltpu.make_async_remote_copy(
                src_ref=buffer.at[source], dst_ref=buffer.at[source],
                send_sem=send_sem.at[distance], recv_sem=recv_sem.at[distance],
                device_id=partner(axis, distance), device_id_type=MESH,
            ).wait_recv()
        value = buffer[0]
        for i in range(1, counts[axis]):
            value = value + buffer[i]
    out_ref[...] = value


def sum_over_devices(local):
    counts = [lax.axis_size(a) for a in ("gx", "gy", "gz")]
    vmem = pl.BlockSpec(memory_space=pltpu.VMEM)
    return pl.pallas_call(
        sum_kernel,
        out_shape=jax.ShapeDtypeStruct(local.shape, jnp.float32),
        in_specs=[vmem],
        out_specs=vmem,
        scratch_shapes=[pltpu.VMEM((n,) + local.shape, jnp.float32) for n in counts]
        + [pltpu.SemaphoreType.DMA((n,)) for n in counts] * 2,
        compiler_params=pltpu.CompilerParams(collective_id=1, has_side_effects=True),
    )(local)


def project_kernel(cells, sums_ref, inverse_ref, projected_ref):
    rows = sums_ref.shape[0]
    sums = sums_ref[...] * (1.0 / cells)
    correlation, energy = sums[:, :rows], sums[:, rows:]
    correlation = 0.5 * (correlation + correlation.T)
    row_index = lax.broadcasted_iota(jnp.int32, (rows, rows), 0)
    column_index = lax.broadcasted_iota(jnp.int32, (rows, rows), 1)
    eye = jnp.where(row_index == column_index, jnp.float32(1.0), jnp.float32(0.0))
    work = jnp.concatenate([correlation, eye], axis=1)
    blocks = [work[i : i + SUB] for i in range(0, rows, SUB)]
    sub = lax.broadcasted_iota(jnp.int32, (SUB, 2 * rows), 0)
    for j in range(rows):
        own, at = divmod(j, SUB)
        columns = {
            b: jnp.broadcast_to(blocks[b][:, j : j + 1], (SUB, 2 * rows))
            for b in range(own, len(blocks))
        }
        ratio = blocks[own][at : at + 1] / columns[own][at : at + 1]
        for b in range(own, len(blocks)):
            updated = blocks[b] - columns[b] * ratio
            blocks[b] = jnp.where(sub > at, updated, blocks[b]) if b == own else updated
    work = jnp.concatenate(blocks, axis=0)
    pivots = jnp.sum(
        jnp.where(row_index == column_index, work[:, :rows], jnp.float32(0.0)),
        axis=1, keepdims=True,
    )
    inverse = work[:, rows:] / jnp.sqrt(pivots)
    inverse_ref[...] = inverse
    half_way = jnp.dot(inverse, energy, precision=lax.Precision.HIGHEST)
    projected_ref[...] = lax.dot_general(
        half_way, inverse, (((1,), (1,)), ((), ())), precision=lax.Precision.HIGHEST
    )


def project(sums, cells):
    rows = sums.shape[0]
    vmem = pl.BlockSpec(memory_space=pltpu.VMEM)
    return pl.pallas_call(
        functools.partial(project_kernel, cells),
        out_shape=[jax.ShapeDtypeStruct((rows, rows), jnp.float32)] * 2,
        in_specs=[vmem],
        out_specs=[vmem] * 2,
    )(sums)


def body(initial_block, phase_map, phase_density, phase_modulus, bloch_sign):
    inv_rho = lookup(phase_map, 1.0 / phase_density)
    kappa = lookup(phase_map, phase_modulus)
    sign = bloch_sign.astype(jnp.float32)
    z_index = lax.axis_index("gz")
    z_count = lax.axis_size("gz")
    low_factor = jnp.where(z_index == 0, sign, jnp.float32(1.0))
    high_factor = jnp.where(z_index == z_count - 1, sign, jnp.float32(1.0))
    top = 12.0 * jnp.max(phase_modulus) * jnp.max(1.0 / phase_density)
    low = 0.03 * top
    centre = (top + low) / 2.0
    half = (top - low) / 2.0
    cells = (
        initial_block.shape[1]
        * initial_block.shape[2]
        * initial_block.shape[3]
        * lax.axis_size("gx")
        * lax.axis_size("gy")
        * z_count
    )
    scal = jnp.stack([2.0 / half, 2.0 * centre / half])
    current, both = filtered_block(scal, initial_block, inv_rho, kappa, low_factor, high_factor)
    rows = current.shape[0]
    flat = current.reshape(rows, -1)
    local = jnp.dot(flat, both.reshape(2 * rows, -1).T, precision=lax.Precision.HIGHEST)
    inverse, projected = project(sum_over_devices(local), cells)
    basis = jnp.dot(inverse, flat, precision=lax.Precision.HIGHEST).reshape(current.shape)
    return (basis, projected)


def solution(mesh):
    in_specs = (P(None, "gz", "gy", "gx"), P("gz", "gy", "gx"), P(), P(), P("gy", "gx"))
    out_specs = (P(None, "gz", "gy", "gx"), P())
    return jax.shard_map(body, mesh=mesh, in_specs=in_specs, out_specs=out_specs, check_vma=False)
```

```python
import functools

import jax
import jax.numpy as jnp
from jax import lax
from jax.experimental import pallas as pl
from jax.experimental.pallas import tpu as pltpu
from jax.sharding import PartitionSpec as P

DEGREE = 6
GROUPS = 4
UNROLL = 2
SUB, LANE = 8, 128
MESH = pl.DeviceIdType.MESH


def filter_kernel(
    density_ref, modulus_ref, init_ref, phase_ref, sign_ref,
    filt_ref, both_ref,
    app_ref, wcoef, vcoef, sendz, sendy, sendx, haloz, haloy, halox, send_sem, recv_sem,
):
    rows, nz = init_ref.shape[0], init_ref.shape[1]
    size = rows // GROUPS
    spans = [(g * size, size) for g in range(GROUPS)] + [(rows, 1)]
    gx, gy, gz = (lax.axis_index(a) for a in ("gx", "gy", "gz"))
    cx, cy, cz = (lax.axis_size(a) for a in ("gx", "gy", "gz"))
    other_x = (lax.rem(gx + 1, cx), gy, gz)
    y_up = (gx, lax.rem(gy + 1, cy), gz)
    y_down = (gx, lax.rem(gy + cy - 1, cy), gz)
    z_up = (gx, gy, lax.rem(gz + 1, cz))
    z_down = (gx, gy, lax.rem(gz + cz - 1, cz))

    barrier = pltpu.get_barrier_semaphore()
    for device in (other_x, y_up, y_down, z_up, z_down):
        pl.semaphore_signal(barrier, inc=1, device_id=device, device_id_type=MESH)
    pl.semaphore_wait(barrier, 5)

    lane = lax.broadcasted_iota(jnp.int32, (SUB, LANE), 1)
    sub = lax.broadcasted_iota(jnp.int32, (SUB, LANE), 0)

    def copies(slot, g, one_way=False):
        start, length = spans[g]
        part = pl.ds(start, length)
        plan = (
            (sendy.at[0, part], haloy.at[slot, 1, part], y_down),
            (sendy.at[1, part], haloy.at[slot, 0, part], y_up),
            (sendz.at[0, part], haloz.at[slot, 1, part], z_down),
            (sendz.at[1, part], haloz.at[slot, 0, part], z_up),
            (sendx.at[part], halox.at[slot, part], other_x),
        )
        return [
            pltpu.make_async_remote_copy(
                src_ref=src, dst_ref=dst,
                send_sem=send_sem.at[g, i], recv_sem=recv_sem.at[slot, g, i],
                device_id=device, device_id_type=MESH,
            )
            for i, (src, dst, device) in enumerate(plan)
            if not (one_way and i in (1, 3))
        ]

    def pack(tiles, k):
        sendz[0, k] = tiles[0]
        sendz[1, k] = tiles[-1]
        packed = jnp.zeros((SUB, LANE), jnp.float32)
        for z, tile in enumerate(tiles):
            sendy[0, k, z : z + 1, :] = tile[0:1]
            sendy[1, k, z : z + 1, :] = tile[SUB - 1 : SUB]
            packed = jnp.where(lane // 2 == z, pltpu.roll(tile, 2 * z + 1, 1), packed)
        sendx[k] = packed

    def neighbours(tiles, k, slot, z, one_way=False):
        tile = tiles[z]
        z_after = tiles[z + 1] if z + 1 < nz else haloz[slot, 1, k]
        y_after = jnp.where(
            sub == SUB - 1, haloy[slot, 1, k, z : z + 1, :], pltpu.roll(tile, SUB - 1, 0)
        )
        edge = pltpu.roll(halox[slot, k], LANE - 2 * z - 1, 1)
        x_after = pltpu.roll(jnp.where(lane == 0, edge, tile), LANE - 1, 1)
        if one_way:
            return z_after, y_after, x_after
        z_before = tiles[z - 1] if z else haloz[slot, 0, k]
        y_before = jnp.where(sub == 0, haloy[slot, 0, k, z : z + 1, :], pltpu.roll(tile, 1, 0))
        x_before = pltpu.roll(jnp.where(lane == LANE - 1, edge, tile), 1, 1)
        return z_after, y_after, x_after, z_before, y_before, x_before

    def send(slot, g, one_way=False):
        for copy in copies(slot, g, one_way):
            copy.start()

    def arrive(slot, g, one_way=False):
        for copy in copies(slot, g, one_way):
            copy.wait()

    def filled(value):
        return jnp.full((SUB, LANE), value, jnp.float32)

    count = density_ref.shape[0]
    densities = [1.0 / filled(density_ref[i]) for i in range(count)]
    moduli = [filled(modulus_ref[i]) for i in range(count)]
    phases = [phase_ref[z] for z in range(nz)]

    def looked_up(phase, table):
        value = jnp.zeros((SUB, LANE), jnp.float32)
        for i, entry in enumerate(table):
            value = jnp.where(phase == i, entry, value)
        return value

    rho = [looked_up(phase, densities) for phase in phases]
    pack(rho, rows)
    send(0, GROUPS)
    for g in range(GROUPS):
        start, length = spans[g]

        def first(i, carry):
            for u in range(UNROLL):
                k = start + i * UNROLL + u
                pack([init_ref[k, z] for z in range(nz)], k)
            return carry

        lax.fori_loop(0, length // UNROLL, first, 0)
        send(0, g)

    top = 12.0 * functools.reduce(jnp.maximum, moduli) * functools.reduce(jnp.maximum, densities)
    low = 0.03 * top
    centre = (top + low) / 2.0
    half = (top - low) / 2.0
    scale, shift = 2.0 / half, 2.0 * centre / half
    sign = sign_ref[...].astype(jnp.float32)
    at_low = jnp.broadcast_to(gz, (SUB, LANE)) == 0
    at_high = jnp.broadcast_to(gz, (SUB, LANE)) == cz - 1
    low_sign = jnp.where(at_low, sign, jnp.float32(1.0))
    high_sign = jnp.where(at_high, sign, jnp.float32(1.0))

    arrive(0, GROUPS)
    for z in range(nz):
        kappa = looked_up(phases[z], moduli)
        weights = [0.5 * (rho[z] + n) for n in neighbours(rho, rows, 0, z)]
        total = weights[0] + weights[3]
        total = total + (weights[1] + weights[4])
        total = total + (weights[2] + weights[5])
        if z == nz - 1:
            weights[0] = weights[0] * high_sign
        if z == 0:
            weights[3] = weights[3] * low_sign
        factor = scale * kappa
        for i, w in enumerate(weights):
            if i < 3:
                wcoef[i, z] = w
            vcoef[i, z] = factor * w
        wcoef[3, z] = 0.5 * total
        wcoef[4, z] = 1.0 / kappa
        vcoef[6, z] = factor * total - shift

    for step in range(DEGREE + 1):
        slot = step % 2
        last = step == DEGREE
        current = init_ref if step == 0 else (app_ref if step % 2 else filt_ref)
        target = app_ref if step % 2 == 0 else filt_ref
        previous = None
        if 0 < step < DEGREE:
            previous = init_ref if step == 1 else target
        for g in range(GROUPS):
            start, length = spans[g]
            arrive(slot, g, last)

            def one(i, carry):
                ks = [start + i * UNROLL + u for u in range(UNROLL)]
                fields = [[current[k, z] for z in range(nz)] for k in ks]
                made = [[] for _ in ks]
                for z in range(nz):
                    for u, k in enumerate(ks):
                        tiles = fields[u]
                        around = neighbours(tiles, k, slot, z, last)
                        if last:
                            terms = [wcoef[j, z] * n for j, n in enumerate(around)]
                            value = wcoef[3, z] * tiles[z] - ((terms[0] + terms[1]) + terms[2])
                        else:
                            terms = [vcoef[j, z] * n for j, n in enumerate(around)]
                            pairs = (terms[0] + terms[3]) + (terms[1] + terms[4])
                            value = vcoef[6, z] * tiles[z] - (pairs + (terms[2] + terms[5]))
                        if step == 0:
                            value = 0.5 * value
                        if previous is not None:
                            value = value - previous[k, z]
                        made[u].append(value)
                for u, k in enumerate(ks):
                    for z in range(nz):
                        if last:
                            both_ref[k, z] = fields[u][z] * wcoef[4, z]
                            both_ref[rows + k, z] = made[u][z]
                        else:
                            target[k, z] = made[u][z]
                    if not last:
                        pack(made[u], k)
                return carry

            lax.fori_loop(0, length // UNROLL, one, 0)
            if not last:
                send(1 - slot, g, step == DEGREE - 1)


def filtered_block(density, modulus, block, phase, sign):
    rows = block.shape[0]
    vmem = pl.BlockSpec(memory_space=pltpu.VMEM)
    nz = block.shape[1]
    f32 = jnp.float32
    return pl.pallas_call(
        filter_kernel,
        out_shape=[
            jax.ShapeDtypeStruct(block.shape, f32),
            jax.ShapeDtypeStruct((2 * rows,) + block.shape[1:], f32),
        ],
        in_specs=[pl.BlockSpec(memory_space=pltpu.SMEM)] * 2 + [vmem] * 3,
        out_specs=[vmem] * 2,
        scratch_shapes=[
            pltpu.VMEM(block.shape, f32),
            pltpu.VMEM((5, nz, SUB, LANE), f32),
            pltpu.VMEM((7, nz, SUB, LANE), f32),
            pltpu.VMEM((2, rows + 1, SUB, LANE), f32),
            pltpu.VMEM((2, rows + 1, SUB, LANE), f32),
            pltpu.VMEM((rows + 1, SUB, LANE), f32),
            pltpu.VMEM((2, 2, rows + 1, SUB, LANE), f32),
            pltpu.VMEM((2, 2, rows + 1, SUB, LANE), f32),
            pltpu.VMEM((2, rows + 1, SUB, LANE), f32),
            pltpu.SemaphoreType.DMA((GROUPS + 1, 5)),
            pltpu.SemaphoreType.DMA((2, GROUPS + 1, 5)),
        ],
        compiler_params=pltpu.CompilerParams(
            collective_id=0, has_side_effects=True, vmem_limit_bytes=40 * 1024 * 1024
        ),
    )(density, modulus, block, phase, sign)


def sum_kernel(local_ref, out_ref, *scratch):
    axes = ("gx", "gy", "gz")
    buffers, sends, arrivals = scratch[:3], scratch[3:6], scratch[6:9]
    places = {a: lax.axis_index(a) for a in axes}
    counts = {a: lax.axis_size(a) for a in axes}

    def partner(axis, distance):
        count = counts[axis]
        place = dict(places)
        place[axis] = lax.rem(places[axis] + distance, count)
        return tuple(place[a] for a in axes)

    barrier = pltpu.get_barrier_semaphore()
    greeted = 0
    for axis in axes:
        for distance in range(1, counts[axis]):
            pl.semaphore_signal(
                barrier, inc=1, device_id=partner(axis, distance), device_id_type=MESH
            )
            greeted += 1
    pl.semaphore_wait(barrier, greeted)

    value = local_ref[...]
    for axis, buffer, send_sem, recv_sem in zip(axes, buffers, sends, arrivals):
        me = places[axis]
        buffer[me] = value
        started = []
        for distance in range(1, counts[axis]):
            copy = pltpu.make_async_remote_copy(
                src_ref=buffer.at[me], dst_ref=buffer.at[me],
                send_sem=send_sem.at[distance], recv_sem=recv_sem.at[distance],
                device_id=partner(axis, distance), device_id_type=MESH,
            )
            copy.start()
            started.append(copy)
        for distance, copy in enumerate(started, 1):
            copy.wait_send()
            source = lax.rem(me + counts[axis] - distance, counts[axis])
            pltpu.make_async_remote_copy(
                src_ref=buffer.at[source], dst_ref=buffer.at[source],
                send_sem=send_sem.at[distance], recv_sem=recv_sem.at[distance],
                device_id=partner(axis, distance), device_id_type=MESH,
            ).wait_recv()
        value = buffer[0]
        for i in range(1, counts[axis]):
            value = value + buffer[i]
    out_ref[...] = value


def sum_over_devices(local):
    counts = [lax.axis_size(a) for a in ("gx", "gy", "gz")]
    vmem = pl.BlockSpec(memory_space=pltpu.VMEM)
    return pl.pallas_call(
        sum_kernel,
        out_shape=jax.ShapeDtypeStruct(local.shape, jnp.float32),
        in_specs=[vmem],
        out_specs=vmem,
        scratch_shapes=[pltpu.VMEM((n,) + local.shape, jnp.float32) for n in counts]
        + [pltpu.SemaphoreType.DMA((n,)) for n in counts] * 2,
        compiler_params=pltpu.CompilerParams(collective_id=1, has_side_effects=True),
    )(local)


def project_kernel(cells, sums_ref, inverse_ref, projected_ref):
    rows = sums_ref.shape[0]
    sums = sums_ref[...] * (1.0 / cells)
    correlation, energy = sums[:, :rows], sums[:, rows:]
    correlation = 0.5 * (correlation + correlation.T)
    energy = energy + energy.T
    row_index = lax.broadcasted_iota(jnp.int32, (rows, rows), 0)
    column_index = lax.broadcasted_iota(jnp.int32, (rows, rows), 1)
    eye = jnp.where(row_index == column_index, jnp.float32(1.0), jnp.float32(0.0))
    work = jnp.concatenate([correlation, eye], axis=1)
    blocks = [work[i : i + SUB] for i in range(0, rows, SUB)]
    sub = lax.broadcasted_iota(jnp.int32, (SUB, 2 * rows), 0)
    for j in range(rows):
        own, at = divmod(j, SUB)
        columns = {
            b: jnp.broadcast_to(blocks[b][:, j : j + 1], (SUB, 2 * rows))
            for b in range(own, len(blocks))
        }
        ratio = blocks[own][at : at + 1] / columns[own][at : at + 1]
        for b in range(own, len(blocks)):
            updated = blocks[b] - columns[b] * ratio
            blocks[b] = jnp.where(sub > at, updated, blocks[b]) if b == own else updated
    work = jnp.concatenate(blocks, axis=0)
    pivots = jnp.sum(
        jnp.where(row_index == column_index, work[:, :rows], jnp.float32(0.0)),
        axis=1, keepdims=True,
    )
    inverse = work[:, rows:] / jnp.sqrt(pivots)
    inverse_ref[...] = inverse
    half_way = jnp.dot(inverse, energy, precision=lax.Precision.HIGHEST)
    projected_ref[...] = lax.dot_general(
        half_way, inverse, (((1,), (1,)), ((), ())), precision=lax.Precision.HIGHEST
    )


def project(sums, cells):
    rows = sums.shape[0]
    vmem = pl.BlockSpec(memory_space=pltpu.VMEM)
    return pl.pallas_call(
        functools.partial(project_kernel, cells),
        out_shape=[jax.ShapeDtypeStruct((rows, rows), jnp.float32)] * 2,
        in_specs=[vmem],
        out_specs=[vmem] * 2,
    )(sums)


def body(initial_block, phase_map, phase_density, phase_modulus, bloch_sign):
    z_count = lax.axis_size("gz")
    cells = (
        initial_block.shape[1]
        * initial_block.shape[2]
        * initial_block.shape[3]
        * lax.axis_size("gx")
        * lax.axis_size("gy")
        * z_count
    )
    current, both = filtered_block(
        phase_density, phase_modulus, initial_block, phase_map, bloch_sign
    )
    rows = current.shape[0]
    flat = current.reshape(rows, -1)
    local = jnp.dot(flat, both.reshape(2 * rows, -1).T, precision=lax.Precision.HIGHEST)
    inverse, projected = project(sum_over_devices(local), cells)
    basis = jnp.dot(inverse, flat, precision=lax.Precision.HIGHEST).reshape(current.shape)
    return (basis, projected)


def solution(mesh):
    in_specs = (P(None, "gz", "gy", "gx"), P("gz", "gy", "gx"), P(), P(), P("gy", "gx"))
    out_specs = (P(None, "gz", "gy", "gx"), P())
    return jax.shard_map(body, mesh=mesh, in_specs=in_specs, out_specs=out_specs, check_vma=False)
```

```python
import functools

import jax
import jax.numpy as jnp
from jax import lax
from jax.experimental import pallas as pl
from jax.experimental.pallas import tpu as pltpu
from jax.sharding import PartitionSpec as P

DEGREE = 6
GROUPS = 4
UNROLL = 2
SUB, LANE = 8, 128
MESH = pl.DeviceIdType.MESH


def filter_kernel(
    density_ref, modulus_ref, init_ref, phase_ref, sign_ref,
    filt_ref, both_ref,
    app_ref, wcoef, vcoef, sendz, sendy, sendx, haloz, haloy, halox, send_sem, recv_sem,
):
    rows, nz = init_ref.shape[0], init_ref.shape[1]
    size = rows // GROUPS
    spans = [(g * size, size) for g in range(GROUPS)] + [(rows, 1)]
    gx, gy, gz = (lax.axis_index(a) for a in ("gx", "gy", "gz"))
    cx, cy, cz = (lax.axis_size(a) for a in ("gx", "gy", "gz"))
    other_x = (lax.rem(gx + 1, cx), gy, gz)
    y_up = (gx, lax.rem(gy + 1, cy), gz)
    y_down = (gx, lax.rem(gy + cy - 1, cy), gz)
    z_up = (gx, gy, lax.rem(gz + 1, cz))
    z_down = (gx, gy, lax.rem(gz + cz - 1, cz))

    barrier = pltpu.get_barrier_semaphore()
    for device in (other_x, y_up, y_down, z_up, z_down):
        pl.semaphore_signal(barrier, inc=1, device_id=device, device_id_type=MESH)
    pl.semaphore_wait(barrier, 5)

    lane = lax.broadcasted_iota(jnp.int32, (SUB, LANE), 1)
    sub = lax.broadcasted_iota(jnp.int32, (SUB, LANE), 0)

    def copies(slot, g, one_way=False):
        start, length = spans[g]
        part = pl.ds(start, length)
        plan = (
            (sendy.at[0, part], haloy.at[slot, 1, part], y_down),
            (sendy.at[1, part], haloy.at[slot, 0, part], y_up),
            (sendz.at[0, part], haloz.at[slot, 1, part], z_down),
            (sendz.at[1, part], haloz.at[slot, 0, part], z_up),
            (sendx.at[part], halox.at[slot, part], other_x),
        )
        return [
            pltpu.make_async_remote_copy(
                src_ref=src, dst_ref=dst,
                send_sem=send_sem.at[g, i], recv_sem=recv_sem.at[slot, g, i],
                device_id=device, device_id_type=MESH,
            )
            for i, (src, dst, device) in enumerate(plan)
            if not (one_way and i in (1, 3))
        ]

    def pack(tiles, k):
        sendz[0, k] = tiles[0]
        sendz[1, k] = tiles[-1]
        packed = jnp.zeros((SUB, LANE), jnp.float32)
        for z, tile in enumerate(tiles):
            sendy[0, k, z : z + 1, :] = tile[0:1]
            sendy[1, k, z : z + 1, :] = tile[SUB - 1 : SUB]
            packed = jnp.where(lane // 2 == z, pltpu.roll(tile, 2 * z + 1, 1), packed)
        sendx[k] = packed

    def neighbours(tiles, k, slot, z, one_way=False):
        tile = tiles[z]
        z_after = tiles[z + 1] if z + 1 < nz else haloz[slot, 1, k]
        y_after = jnp.where(
            sub == SUB - 1, haloy[slot, 1, k, z : z + 1, :], pltpu.roll(tile, SUB - 1, 0)
        )
        edge = pltpu.roll(halox[slot, k], LANE - 2 * z - 1, 1)
        x_after = pltpu.roll(jnp.where(lane == 0, edge, tile), LANE - 1, 1)
        if one_way:
            return z_after, y_after, x_after
        z_before = tiles[z - 1] if z else haloz[slot, 0, k]
        y_before = jnp.where(sub == 0, haloy[slot, 0, k, z : z + 1, :], pltpu.roll(tile, 1, 0))
        x_before = pltpu.roll(jnp.where(lane == LANE - 1, edge, tile), 1, 1)
        return z_after, y_after, x_after, z_before, y_before, x_before

    def send(slot, g, one_way=False):
        for copy in copies(slot, g, one_way):
            copy.start()

    def arrive(slot, g, one_way=False):
        for copy in copies(slot, g, one_way):
            copy.wait()

    def filled(value):
        return jnp.full((SUB, LANE), value, jnp.float32)

    count = density_ref.shape[0]
    densities = [1.0 / filled(density_ref[i]) for i in range(count)]
    moduli = [filled(modulus_ref[i]) for i in range(count)]
    phases = [phase_ref[z] for z in range(nz)]

    def looked_up(phase, table):
        value = jnp.zeros((SUB, LANE), jnp.float32)
        for i, entry in enumerate(table):
            value = jnp.where(phase == i, entry, value)
        return value

    rho = [looked_up(phase, densities) for phase in phases]
    pack(rho, rows)
    send(0, GROUPS)
    for g in range(GROUPS):
        start, length = spans[g]

        def first(i, carry):
            for u in range(UNROLL):
                k = start + i * UNROLL + u
                pack([init_ref[k, z] for z in range(nz)], k)
            return carry

        lax.fori_loop(0, length // UNROLL, first, 0)
        send(0, g)

    top = 12.0 * functools.reduce(jnp.maximum, moduli) * functools.reduce(jnp.maximum, densities)
    low = 0.03 * top
    centre = (top + low) / 2.0
    half = (top - low) / 2.0
    scale, shift = 2.0 / half, 2.0 * centre / half
    sign = sign_ref[...].astype(jnp.float32)
    at_low = jnp.broadcast_to(gz, (SUB, LANE)) == 0
    at_high = jnp.broadcast_to(gz, (SUB, LANE)) == cz - 1
    low_sign = jnp.where(at_low, sign, jnp.float32(1.0))
    high_sign = jnp.where(at_high, sign, jnp.float32(1.0))

    arrive(0, GROUPS)
    for z in range(nz):
        kappa = looked_up(phases[z], moduli)
        weights = [0.5 * (rho[z] + n) for n in neighbours(rho, rows, 0, z)]
        total = weights[0] + weights[3]
        total = total + (weights[1] + weights[4])
        total = total + (weights[2] + weights[5])
        if z == nz - 1:
            weights[0] = weights[0] * high_sign
        if z == 0:
            weights[3] = weights[3] * low_sign
        factor = scale * kappa
        for i, w in enumerate(weights):
            if i < 3:
                wcoef[i, z] = w
            vcoef[i, z] = factor * w
        wcoef[3, z] = 0.5 * total
        wcoef[4, z] = 1.0 / kappa
        vcoef[6, z] = factor * total - shift

    for step in range(DEGREE + 1):
        slot = step % 2
        last = step == DEGREE
        current = init_ref if step == 0 else (app_ref if step % 2 else filt_ref)
        target = app_ref if step % 2 == 0 else filt_ref
        previous = None
        if 0 < step < DEGREE:
            previous = init_ref if step == 1 else target
        for g in range(GROUPS):
            start, length = spans[g]
            arrive(slot, g, last)

            def one(i, carry):
                ks = [start + i * UNROLL + u for u in range(UNROLL)]
                fields = [[current[k, z] for z in range(nz)] for k in ks]
                made = [[] for _ in ks]
                for z in range(nz):
                    for u, k in enumerate(ks):
                        tiles = fields[u]
                        around = neighbours(tiles, k, slot, z, last)
                        if last:
                            terms = [wcoef[j, z] * n for j, n in enumerate(around)]
                            value = wcoef[3, z] * tiles[z] - ((terms[0] + terms[1]) + terms[2])
                        else:
                            terms = [vcoef[j, z] * n for j, n in enumerate(around)]
                            pairs = (terms[0] + terms[3]) + (terms[1] + terms[4])
                            value = vcoef[6, z] * tiles[z] - (pairs + (terms[2] + terms[5]))
                        if step == 0:
                            value = 0.5 * value
                        if previous is not None:
                            value = value - previous[k, z]
                        made[u].append(value)
                for u, k in enumerate(ks):
                    for z in range(nz):
                        if last:
                            both_ref[k, z] = fields[u][z] * wcoef[4, z]
                            both_ref[rows + k, z] = made[u][z]
                        else:
                            target[k, z] = made[u][z]
                    if not last:
                        pack(made[u], k)
                return carry

            lax.fori_loop(0, length // UNROLL, one, 0)
            if not last:
                send(1 - slot, g, step == DEGREE - 1)


def filtered_block(density, modulus, block, phase, sign):
    rows = block.shape[0]
    vmem = pl.BlockSpec(memory_space=pltpu.VMEM)
    nz = block.shape[1]
    f32 = jnp.float32
    return pl.pallas_call(
        filter_kernel,
        out_shape=[
            jax.ShapeDtypeStruct(block.shape, f32),
            jax.ShapeDtypeStruct((2 * rows,) + block.shape[1:], f32),
        ],
        in_specs=[pl.BlockSpec(memory_space=pltpu.SMEM)] * 2 + [vmem] * 3,
        out_specs=[vmem] * 2,
        scratch_shapes=[
            pltpu.VMEM(block.shape, f32),
            pltpu.VMEM((5, nz, SUB, LANE), f32),
            pltpu.VMEM((7, nz, SUB, LANE), f32),
            pltpu.VMEM((2, rows + 1, SUB, LANE), f32),
            pltpu.VMEM((2, rows + 1, SUB, LANE), f32),
            pltpu.VMEM((rows + 1, SUB, LANE), f32),
            pltpu.VMEM((2, 2, rows + 1, SUB, LANE), f32),
            pltpu.VMEM((2, 2, rows + 1, SUB, LANE), f32),
            pltpu.VMEM((2, rows + 1, SUB, LANE), f32),
            pltpu.SemaphoreType.DMA((GROUPS + 1, 5)),
            pltpu.SemaphoreType.DMA((2, GROUPS + 1, 5)),
        ],
        compiler_params=pltpu.CompilerParams(
            collective_id=0, has_side_effects=True, vmem_limit_bytes=40 * 1024 * 1024
        ),
    )(density, modulus, block, phase, sign)


def sum_kernel(cells, local_ref, inverse_ref, projected_ref, *scratch):
    axes = ("gx", "gy", "gz")
    buffers, sends, arrivals = scratch[:3], scratch[3:6], scratch[6:9]
    places = {a: lax.axis_index(a) for a in axes}
    counts = {a: lax.axis_size(a) for a in axes}

    def partner(axis, distance):
        count = counts[axis]
        place = dict(places)
        place[axis] = lax.rem(places[axis] + distance, count)
        return tuple(place[a] for a in axes)

    barrier = pltpu.get_barrier_semaphore()
    greeted = 0
    for axis in axes:
        for distance in range(1, counts[axis]):
            pl.semaphore_signal(
                barrier, inc=1, device_id=partner(axis, distance), device_id_type=MESH
            )
            greeted += 1
    pl.semaphore_wait(barrier, greeted)

    value = local_ref[...]
    for axis, buffer, send_sem, recv_sem in zip(axes, buffers, sends, arrivals):
        me = places[axis]
        buffer[me] = value
        started = []
        for distance in range(1, counts[axis]):
            copy = pltpu.make_async_remote_copy(
                src_ref=buffer.at[me], dst_ref=buffer.at[me],
                send_sem=send_sem.at[distance], recv_sem=recv_sem.at[distance],
                device_id=partner(axis, distance), device_id_type=MESH,
            )
            copy.start()
            started.append(copy)
        for distance, copy in enumerate(started, 1):
            copy.wait_send()
            source = lax.rem(me + counts[axis] - distance, counts[axis])
            pltpu.make_async_remote_copy(
                src_ref=buffer.at[source], dst_ref=buffer.at[source],
                send_sem=send_sem.at[distance], recv_sem=recv_sem.at[distance],
                device_id=partner(axis, distance), device_id_type=MESH,
            ).wait_recv()
        value = buffer[0]
        for i in range(1, counts[axis]):
            value = value + buffer[i]
    project_sums(cells, value, inverse_ref, projected_ref)


def sum_and_project(local, cells):
    rows = local.shape[0]
    counts = [lax.axis_size(a) for a in ("gx", "gy", "gz")]
    vmem = pl.BlockSpec(memory_space=pltpu.VMEM)
    return pl.pallas_call(
        functools.partial(sum_kernel, cells),
        out_shape=[jax.ShapeDtypeStruct((rows, rows), jnp.float32)] * 2,
        in_specs=[vmem],
        out_specs=[vmem] * 2,
        scratch_shapes=[pltpu.VMEM((n,) + local.shape, jnp.float32) for n in counts]
        + [pltpu.SemaphoreType.DMA((n,)) for n in counts] * 2,
        compiler_params=pltpu.CompilerParams(collective_id=1, has_side_effects=True),
    )(local)


def project_sums(cells, sums, inverse_ref, projected_ref):
    rows = sums.shape[0]
    sums = sums * (1.0 / cells)
    correlation, energy = sums[:, :rows], sums[:, rows:]
    correlation = 0.5 * (correlation + correlation.T)
    energy = energy + energy.T
    row_index = lax.broadcasted_iota(jnp.int32, (rows, rows), 0)
    column_index = lax.broadcasted_iota(jnp.int32, (rows, rows), 1)
    eye = jnp.where(row_index == column_index, jnp.float32(1.0), jnp.float32(0.0))
    work = jnp.concatenate([correlation, eye], axis=1)
    blocks = [work[i : i + SUB] for i in range(0, rows, SUB)]
    sub = lax.broadcasted_iota(jnp.int32, (SUB, 2 * rows), 0)
    for j in range(rows):
        own, at = divmod(j, SUB)
        columns = {
            b: jnp.broadcast_to(blocks[b][:, j : j + 1], (SUB, 2 * rows))
            for b in range(own, len(blocks))
        }
        ratio = blocks[own][at : at + 1] / columns[own][at : at + 1]
        for b in range(own, len(blocks)):
            updated = blocks[b] - columns[b] * ratio
            blocks[b] = jnp.where(sub > at, updated, blocks[b]) if b == own else updated
    work = jnp.concatenate(blocks, axis=0)
    pivots = jnp.sum(
        jnp.where(row_index == column_index, work[:, :rows], jnp.float32(0.0)),
        axis=1, keepdims=True,
    )
    inverse = work[:, rows:] / jnp.sqrt(pivots)
    inverse_ref[...] = inverse
    half_way = jnp.dot(inverse, energy, precision=lax.Precision.HIGHEST)
    projected_ref[...] = lax.dot_general(
        half_way, inverse, (((1,), (1,)), ((), ())), precision=lax.Precision.HIGHEST
    )


def body(initial_block, phase_map, phase_density, phase_modulus, bloch_sign):
    z_count = lax.axis_size("gz")
    cells = (
        initial_block.shape[1]
        * initial_block.shape[2]
        * initial_block.shape[3]
        * lax.axis_size("gx")
        * lax.axis_size("gy")
        * z_count
    )
    current, both = filtered_block(
        phase_density, phase_modulus, initial_block, phase_map, bloch_sign
    )
    rows = current.shape[0]
    flat = current.reshape(rows, -1)
    local = jnp.dot(flat, both.reshape(2 * rows, -1).T, precision=lax.Precision.HIGHEST)
    inverse, projected = sum_and_project(local, cells)
    basis = jnp.dot(inverse, flat, precision=lax.Precision.HIGHEST).reshape(current.shape)
    return (basis, projected)


def solution(mesh):
    in_specs = (P(None, "gz", "gy", "gx"), P("gz", "gy", "gx"), P(), P(), P("gy", "gx"))
    out_specs = (P(None, "gz", "gy", "gx"), P())
    return jax.shard_map(body, mesh=mesh, in_specs=in_specs, out_specs=out_specs, check_vma=False)
```
